32 devices in a mesh: sector: 8 (over z, y), mpo: 4 (over x, core).
Axes of the slice: x: 2, y: 2, z: 4, core: 2. Of those that a mesh axis runs over, the one named last changes fastest.
Arguments:
- psi: bfloat16 [16, 128, 2048], P('sector', 'mpo'), may hold values from -150 to 150
- left_env: bfloat16 [16, 128, 128, 128], P('sector', 'mpo'), may hold values from -0.5 to 0.5
- right_env: bfloat16 [16, 128, 128, 128], P('sector', 'mpo'), may hold values from -0.046875 to 0.046875
- term_op: int32 [128], P('mpo'), may hold values from 0 to 7
- ops: bfloat16 [8, 16, 16], replicated, may hold values from -1.5 to 1.5
- energy: float32 [16], replicated, may hold values from -2 to 2
- charge: int32 [16], P('sector'), may hold values from 0 to 15
- block_dims: int32 [16, 2], P('sector'), may hold values from 64 to 128, as said below
- basis: float32 [3, 16, 128, 2048], P(None, 'sector', 'mpo'), may hold values from -0.0029296875 to 0.0029296875
Outputs:
- hpsi: float32 [16, 128, 2048], P('sector', 'mpo')
- correction: float32 [16, 128, 2048], P('sector', 'mpo')
- ritz: float32 [], replicated
- subspace_row: float32 [3], replicated
The draws below stay inside these ranges and needn't reach their ends.
Inputs may be any that keep to these rules, and one draw needn't show every extreme that they name: block_dims[s, 0] rows and block_dims[s, 1] columns of each padded block are valid; some block is full.
All inputs are finite; a program needn't handle non-finite values.
Results may differ from the reference program's by a relative error of at most 0.002.
Values may be sent and summed in bfloat16 or wider, within the bound.
A program may use at most 64 MiB of HBM per device.

```python
import math
import jax
import jax.numpy as jnp
from jax import lax

BLK = 128
P_SIZE = 16
NOPS = 8
NCHARGE = 16
NB = 3
NSEC = 16
K = 128


def draw_psi(key, part):
    keys = jax.random.split(key, 3)
    width = P_SIZE * BLK
    block_pos = jnp.arange(NSEC, dtype=jnp.float32) / max(NSEC - 1, 1)
    block_scale = jnp.exp(jnp.log(3.0) * block_pos)[:, None, None]
    row_scale = jnp.exp(jax.random.uniform(keys[1], (NSEC, BLK, 1), jnp.float32, jnp.log(0.3), jnp.log(3.0)))
    col_scale = jnp.exp(jax.random.uniform(keys[2], (NSEC, 1, width), jnp.float32, jnp.log(0.3), jnp.log(3.0)))
    base = jnp.clip(jax.random.normal(keys[0], (NSEC, BLK, width), jnp.float32), -4.0, 4.0)
    values = base * block_scale * row_scale * col_scale
    return values.astype(jnp.bfloat16)


def draw_block_dims(key, part):
    dims = jax.random.randint(jax.random.fold_in(key, 11), (NSEC, 2), BLK // 2, BLK + 1, dtype=jnp.int32)
    full_at = jax.random.randint(jax.random.fold_in(key, 12), (), 0, NSEC, dtype=jnp.int32)
    least_at = jax.random.randint(jax.random.fold_in(key, 13), (), 0, NSEC, dtype=jnp.int32)
    dims = dims.at[least_at].set(BLK // 2)
    return dims.at[full_at].set(BLK)


def with_ends(result, key, low, largest):
    shape = result.shape
    spot = [jax.random.randint(jax.random.fold_in(key, axis), (), 0, shape[axis]) for axis in range(len(shape))]
    result = result.at[tuple(spot)].set(low)
    longest = shape.index(max(shape))
    spot[longest] = (spot[longest] + 1) % shape[longest]
    return result.at[tuple(spot)].set(largest)


def level_of(own_key, extent, pieces, low, high):
    gain = 1.0
    for axis_at, parts in pieces:
        draws = jax.random.uniform(jax.random.fold_in(jax.random.fold_in(own_key, 6), axis_at), (parts,), jnp.float32, low / len(pieces), high / len(pieces))
        gain = gain * jnp.repeat(jnp.exp(draws), extent[axis_at] // parts).reshape((-1,) + (1,) * (len(extent) - 1 - axis_at))
    return gain


def gaussian(own_key, shape, spread, limit, cuts=(), held_as=jnp.bfloat16):
    loudness = level_of(own_key, shape, cuts, -0.22, 0.18) if cuts else 1.0
    entries = jax.random.normal(own_key, shape, jnp.float32) * spread * loudness
    return jnp.minimum(jnp.maximum(entries, -limit), limit).astype(held_as)


def setup_inputs(seed: int = 0) -> dict:
    key_of = jax.random.split(jax.random.key(seed), 10)
    return {
        "psi": draw_psi(jax.random.fold_in(key_of[9], 71), 0),
        "left_env": gaussian(key_of[1], (NSEC, K, BLK, BLK), BLK ** -0.5, 0.5, ((0, 8), (1, 4))),
        "right_env": gaussian(key_of[2], (NSEC, K, BLK, BLK), (BLK * K) ** -0.5, 0.046875, ((0, 8), (1, 4))),
        "term_op": with_ends(jax.random.randint(key_of[3], (K,), 0, NOPS), jax.random.fold_in(key_of[3], 1), 0, NOPS - 1).astype(jnp.int32),
        "ops": gaussian(key_of[4], (NOPS, P_SIZE, P_SIZE), P_SIZE ** -0.5, 1.5),
        "energy": jnp.clip(jax.random.uniform(key_of[5], (NCHARGE,), jnp.float32, -2.0, 2.0), -2.0, 2.0),
        "charge": with_ends(jax.random.randint(key_of[6], (NSEC,), 0, NCHARGE), jax.random.fold_in(key_of[6], 1), 0, NCHARGE - 1).astype(jnp.int32),
        "block_dims": draw_block_dims(jax.random.fold_in(key_of[9], 71), 0),
        "basis": gaussian(key_of[8], (NB, NSEC, BLK, P_SIZE * BLK), (1.0 / (NSEC * BLK * P_SIZE * BLK) ** 0.5), 0.0029296875, ((1, 8), (2, 4)), jnp.float32),
    }


def sector_mask(block_dims, row_first, row_total, block_size, width):
    rows_ok = (row_first + jnp.arange(row_total, dtype=jnp.int32))[None, :, None] < block_dims[:, 0][:, None, None]
    cols_ok = (jnp.arange(width, dtype=jnp.int32) % block_size)[None, None, :] < block_dims[:, 1][:, None, None]
    return rows_ok & cols_ok

def reference(psi, left_env, right_env, term_op, ops, energy, charge, block_dims, basis):
    width = P_SIZE * BLK
    mask = sector_mask(block_dims, 0, BLK, BLK, width)
    masked = jnp.where(mask, psi, jnp.zeros_like(psi))
    op_mats = ops[term_op]
    level = energy[charge]
    group = math.gcd(K, 4)

    def per_block(items):
        block_x, block_left, block_right = items
        block_f = block_x.astype(jnp.float32)

        def one_group(running, offset):
            left_part = lax.dynamic_slice_in_dim(block_left, offset, group, 0).astype(jnp.float32)
            right_part = lax.dynamic_slice_in_dim(block_right, offset, group, 0).astype(jnp.float32)
            op_part = lax.dynamic_slice_in_dim(op_mats, offset, group, 0).astype(jnp.float32)
            moved = jnp.einsum('kac,cq->kaq', left_part, block_f).astype(jnp.bfloat16)
            moved = moved.astype(jnp.float32).reshape(group, BLK, P_SIZE, BLK)
            mixed = jnp.einsum('kpq,kaqb->kapb', op_part, moved).astype(jnp.bfloat16)
            running = running + jnp.einsum('kapc,kcb->apb', mixed.astype(jnp.float32), right_part)
            return (running, None)
        offsets = jnp.arange(K // group, dtype=jnp.int32) * group
        running, _ = lax.scan(one_group, jnp.zeros((BLK, P_SIZE, BLK), jnp.float32), offsets)
        return running.reshape(BLK, width)
    core = lax.map(per_block, (masked, left_env, right_env))
    masked_f = masked.astype(jnp.float32)
    hpsi = jnp.where(mask, level[:, None, None] * masked_f + core, jnp.zeros_like(core))
    self_sq = jnp.sum(masked_f * masked_f)
    cross = jnp.sum(masked_f * hpsi)
    ritz = cross / (self_sq + 1e-06)
    subspace_row = lax.optimization_barrier(jnp.sum(basis * hpsi[None], axis=(1, 2, 3)))
    resid = hpsi - ritz * masked_f
    resid_sq = jnp.sum(resid * resid)
    correction = resid / jnp.sqrt(resid_sq / (NSEC * BLK * P_SIZE * BLK) + 1e-06)
    return (hpsi, correction, ritz, subspace_row)
```

```python
import functools

import jax
import jax.numpy as jnp
from jax import lax
from jax.experimental import pallas as pl
from jax.experimental.pallas import tpu as pltpu
from jax.sharding import PartitionSpec as P

MESH = pl.DeviceIdType.MESH
F32, BF16, I32 = jnp.float32, jnp.bfloat16, jnp.int32
SUB = 8
CHUNKS = 2
PARTS = 4


def term_table(op_ref, terms, pairs):
    lane = lax.broadcasted_iota(I32, (terms, 128), 1)
    sub = lax.broadcasted_iota(I32, (terms, 128), 0)
    lane1 = lax.broadcasted_iota(I32, (1, 128), 1)
    col = jnp.zeros((terms, 128), I32)
    row = jnp.full((1, 128), -1, I32)
    for k in range(terms):
        o = op_ref[k]
        col = jnp.where(sub == k, o, col)
        row = jnp.where(lane1 == k, o, row)
    row = jnp.broadcast_to(row, (terms, 128))
    one, zero = jnp.ones((terms, 128), I32), jnp.zeros((terms, 128), I32)

    def along(mask, axis):
        return jnp.sum(jnp.where(mask, one, zero), axis=axis, keepdims=True)

    same = col == row
    rank_col = jnp.broadcast_to(along(same & (lane < sub), 1), (terms, 128))
    rank_row = jnp.broadcast_to(along(same & (sub < lane), 0), (terms, 128))
    heads = (row >= 0) & ((rank_row & 1) == 0)
    base = jnp.broadcast_to(along((row < col) & heads, 1), (terms, 128))
    place = 2 * base + rank_col
    hit = place == lane
    index = jnp.sum(jnp.where(hit, sub, zero), axis=0, keepdims=True)
    valid = along(hit, 0) > 0
    start = along(hit & (rank_col == 0), 0) > 0
    even = (rank_col & 1) == 0
    own = along(even & (col == lane), 0)
    upto = along(even & (col <= lane), 0)
    right = jnp.where(valid, index, terms)
    prev = jnp.where(valid & jnp.logical_not(start), (lane1 >> 1) - 1, pairs)
    last = jnp.where(own > 0, upto - 1, pairs)
    return jnp.concatenate([index, right, prev, last, jnp.zeros((4, 128), I32)], axis=0)


def mixing(ops_ref, om_ref):
    op_count, size_p, _ = ops_ref.shape
    wide = size_p * SUB
    up = (
        lax.broadcasted_iota(I32, (wide, size_p), 0) // SUB
        == lax.broadcasted_iota(I32, (wide, size_p), 1)
    ).astype(F32).astype(BF16)
    across = (
        lax.broadcasted_iota(I32, (size_p, wide), 1) // SUB
        == lax.broadcasted_iota(I32, (size_p, wide), 0)
    ).astype(F32).astype(BF16)
    diagonal = (lax.broadcasted_iota(I32, (wide, wide), 0) % SUB) == (
        lax.broadcasted_iota(I32, (wide, wide), 1) % SUB
    )
    for o in range(op_count):
        t = jnp.dot(up, ops_ref[o], preferred_element_type=F32).astype(BF16)
        u = jnp.dot(t, across, preferred_element_type=F32)
        u = jnp.where(diagonal, u, jnp.zeros_like(u)).astype(BF16)
        om_ref[:, o * wide : (o + 1) * wide] = u
        om_ref[:, (op_count + o) * wide : (op_count + o + 1) * wide] = u


def merge(stats, nb):
    xx, xh = stats[:, 0:1], stats[:, 1:2]
    rr, xr = stats[:, 2 + nb : 3 + nb], stats[:, 3 + nb : 4 + nb]
    q = xh / (xx + 1e-6)
    total = jnp.sum(stats, axis=0)
    all_q = total[1:2] / (total[0:1] + 1e-6)
    gap = q - all_q[None]
    rr = jnp.sum(rr + 2.0 * gap * xr + gap * gap * xx, axis=0)
    xr = jnp.sum(xr + gap * xx, axis=0)
    return jnp.concatenate(
        [total[: 2 + nb], rr, xr, jnp.zeros((4 - nb, total.shape[1]), F32)], axis=0
    ), all_q


def kernel(
    n,
    groups,
    cells,
    pairs,
    dims_ref,
    charge_ref,
    energy_ref,
    op_ref,
    ops_ref,
    psi_hbm,
    left_hbm,
    right_hbm,
    basis_hbm,
    hpsi_ref,
    corr_ref,
    stat_ref,
    xraw,
    xt,
    lraw,
    rraw,
    lt,
    rt,
    v_ref,
    sums,
    om_ref,
    turned,
    part_ref,
    theirs,
    away,
    landed,
    basis_ref,
    tab_v,
    tab,
    slots_m,
    slots_s,
    tile,
    own_sem,
    env_sem,
    basis_sem,
    tab_sem,
    gsend,
    grecv,
    fsend,
    frecv,
    send1,
    recv1,
    send2,
    recv2,
    send3,
    recv3,
):
    row = lax.axis_index("sector")
    me = lax.axis_index("mpo")
    chips = n // 2
    core, chip = lax.rem(me, 2), lax.div(me, 2)
    sib = chip * 2 + 1 - core
    sectors, terms, blk, _ = lraw.shape
    rows, cw = xraw.shape[3:]
    size_p = part_ref.shape[1]
    op_count = ops_ref.shape[0]
    nb = basis_ref.shape[0]
    qn = cw // blk
    pn = size_p // PARTS
    width = size_p * blk

    def at(hop):
        return lax.rem(chip + hop, chips) * 2

    envs = {}
    for s in range(sectors):
        envs[0, s] = pltpu.make_async_copy(left_hbm.at[s], lraw.at[s], env_sem.at[0, s])
        envs[1, s] = pltpu.make_async_copy(right_hbm.at[s], rraw.at[s], env_sem.at[1, s])
    own = {}
    for s in range(sectors):
        for c in range(CHUNKS):
            own[s, c] = pltpu.make_async_copy(
                psi_hbm.at[s, :, pl.ds(c * cw, cw)], xraw.at[s, c, me], own_sem.at[s, c]
            )
    barrier = pltpu.get_barrier_semaphore()
    for j in range(1, n):
        pl.semaphore_signal(
            barrier, inc=1, device_id=(row, lax.rem(me + j, n)), device_id_type=MESH
        )
    for j in range(1, groups):
        pl.semaphore_signal(
            barrier, inc=1, device_id=(lax.rem(row + j, groups), me), device_id_type=MESH
        )
    envs[0, 0].start()
    for copy in own.values():
        copy.start()
    envs[1, 0].start()
    for s in range(1, sectors):
        envs[0, s].start()
        envs[1, s].start()
    tab_v[...] = term_table(op_ref, terms, pairs)
    table = pltpu.make_async_copy(tab_v, tab, tab_sem)
    table.start()
    pl.semaphore_wait(barrier, n + groups - 2)

    def push(src, block, s, c, to, ssem, rsem):
        return pltpu.make_async_remote_copy(
            src_ref=src,
            dst_ref=xraw.at[s, c, block],
            send_sem=ssem,
            recv_sem=rsem,
            device_id=(row, to),
            device_id_type=MESH,
        )

    far, near, relay = {}, {}, {}
    for s in range(sectors):
        for c in range(CHUNKS):
            i = s * CHUNKS + c
            src = psi_hbm.at[s, :, pl.ds(c * cw, cw)]
            for hop in range(1, chips):
                far[hop, s, c] = push(
                    src, me, s, c, at(hop) + core, gsend.at[hop, i], grecv.at[hop, i]
                )
                far[hop, s, c].start()
            near[s, c] = push(src, me, s, c, sib, gsend.at[0, i], grecv.at[0, i])
            near[s, c].start()

    def pass_on(s, c):
        i = s * CHUNKS + c
        for hop in range(1, chips):
            far[hop, s, c].wait_recv()
            block = at(chips - hop) + core
            relay[hop, s, c] = push(
                xraw.at[s, c, block], block, s, c, sib, fsend.at[hop, i], frecv.at[hop, i]
            )
            relay[hop, s, c].start()

    def arrived(s, c):
        own[s, c].wait()
        near[s, c].wait_recv()
        for hop in range(1, chips):
            relay[hop, s, c].wait_recv()

    basis_copy = pltpu.make_async_copy(basis_hbm, basis_ref, basis_sem)
    basis_copy.start()
    sums[pairs] = jnp.zeros(sums.shape[1:], F32)

    def turn_left(s):
        envs[0, s].wait()

        def step(i, c):
            for u in range(4):
                k = i * 4 + u
                lt[s, :, pl.ds(pl.multiple_of(k * blk, blk), blk)] = lraw[s, k].T
            return c

        lax.fori_loop(0, terms // 4, step, 0)

    def turn_right(s):
        envs[1, s].wait()

        def step(i, c):
            for u in range(4):
                rt[s, i * 4 + u] = rraw[s, i * 4 + u].T
            return c

        lax.fori_loop(0, terms // 4, step, 0)
        rt[s, terms] = jnp.zeros((blk, blk), BF16)

    turn_left(0)
    pass_on(0, 0)
    mixing(ops_ref, om_ref)
    turn_right(0)
    for c in range(1, CHUNKS):
        pass_on(0, c)
    for s in range(1, sectors):
        turn_left(s)
        turn_right(s)
    table.wait()

    row_at = lax.broadcasted_iota(I32, (blk, blk), 0)
    col_at = lax.broadcasted_iota(I32, (blk, blk), 1)

    def assemble(s, c):
        arrived(s, c)
        ok = (row_at < dims_ref[s, 0]) & (col_at < dims_ref[s, 1])
        for q in range(qn):
            x = jnp.concatenate(
                [xraw[s, c, b, :, q * blk : (q + 1) * blk].astype(F32) for b in range(n)], axis=0
            )
            x = jnp.where(ok, x, jnp.zeros_like(x)).astype(BF16)
            xt[(c * qn + q) * blk : (c * qn + q + 1) * blk, :] = x.T

    def first(s, c):
        def step(i, carry):
            m = jnp.dot(
                xt[c * cw : (c + 1) * cw, :],
                lt[s, :, pl.ds(pl.multiple_of(i * 8 * blk, 8 * blk), 8 * blk)],
                preferred_element_type=F32,
            ).astype(BF16)
            for u in range(8):
                for q in range(qn):
                    v_ref[i * 8 + u, :, (c * qn + q) * blk : (c * qn + q + 1) * blk] = m[
                        q * blk : (q + 1) * blk, u * blk : (u + 1) * blk
                    ]
            return carry

        lax.fori_loop(0, terms // 8, step, 0)

    def second(s):
        def step(i, carry):
            for u in range(4):
                j = i * 4 + u
                r = jnp.concatenate([rt[s, tab[1, 2 * j]], rt[s, tab[1, 2 * j + 1]]], axis=1)
                v = jnp.concatenate([v_ref[tab[0, 2 * j]], v_ref[tab[0, 2 * j + 1]]], axis=0)
                m = jnp.dot(r, v, preferred_element_type=F32)
                prev = tab[2, 2 * j]
                for q in range(size_p):
                    sums[j, q] = sums[prev, q] + m[:, q * blk : (q + 1) * blk]
            return carry

        lax.fori_loop(0, pairs // 4, step, 0)

    def mix():
        wide = size_p * SUB

        def step(i, carry):
            both = []
            for t in range(4):
                b0 = pl.multiple_of((i * 4 + t) * SUB, SUB)
                high, low = [], []
                for o in range(op_count):
                    y = sums[tab[3, o], :, pl.ds(b0, SUB), :].reshape(wide, blk)
                    h = y.astype(BF16)
                    high.append(h)
                    low.append((y - h.astype(F32)).astype(BF16))
                both.append(jnp.concatenate(high + low, axis=0))
            m = jnp.dot(om_ref[...], jnp.concatenate(both, axis=1), preferred_element_type=F32)
            for t in range(4):
                b0 = pl.multiple_of((i * 4 + t) * SUB, SUB)
                turned[:, pl.ds(b0, SUB), :] = m[:, t * blk : (t + 1) * blk].reshape(
                    size_p, SUB, blk
                )
            return carry

        lax.fori_loop(0, blk // (4 * SUB), step, 0)

    order = list(range(1, chips)) + [0]
    swaps, sends = {}, {}

    def rows_of(block):
        return pl.ds(pl.multiple_of(block * rows, rows), rows)

    def turn_out(s):
        for g in range(PARTS):
            for p in range(g * pn, (g + 1) * pn):
                part_ref[s, p] = turned[p].T
            for hop in order:
                swaps[hop, s, g] = pltpu.make_async_remote_copy(
                    src_ref=part_ref.at[s, pl.ds(g * pn, pn), rows_of(at(hop) + 1 - core)],
                    dst_ref=theirs.at[hop, s, g],
                    send_sem=send1.at[hop, s * PARTS + g],
                    recv_sem=recv1.at[hop, s * PARTS + g],
                    device_id=(row, sib),
                    device_id_type=MESH,
                )
                swaps[hop, s, g].start()

    def send_far(s):
        for g in range(PARTS):
            for hop in range(1, chips):
                swaps[hop, s, g].wait_recv()
                y = part_ref[s, g * pn : (g + 1) * pn, rows_of(at(hop) + core), :] + theirs[hop, s, g]
                away[hop - 1, s, g] = y.reshape(pn * rows, blk).astype(BF16)
                sends[hop, s, g] = pltpu.make_async_remote_copy(
                    src_ref=away.at[hop - 1, s, g],
                    dst_ref=landed.at[hop - 1, s, g],
                    send_sem=send2.at[hop, s * PARTS + g],
                    recv_sem=recv2.at[hop, s * PARTS + g],
                    device_id=(row, at(hop) + core),
                    device_id_type=MESH,
                )
                sends[hop, s, g].start()

    zero = jnp.zeros((rows, blk), F32)
    mine_row = me * rows + lax.broadcasted_iota(I32, (rows, blk), 0)
    mine_col = lax.broadcasted_iota(I32, (rows, blk), 1)

    def finish(s, acc):
        xx, xh, bh = acc
        ok = (mine_row < dims_ref[s, 0]) & (mine_col < dims_ref[s, 1])
        level = energy_ref[charge_ref[s]]
        for g in range(PARTS):
            swaps[0, s, g].wait_recv()
            for hop in range(1, chips):
                sends[hop, s, g].wait_recv()
            for u in range(pn):
                p = g * pn + u
                c, q = p // qn, p % qn
                y = part_ref[s, p, rows_of(me), :] + theirs[0, s, g, u]
                for hop in range(1, chips):
                    y = y + landed[hop - 1, s, g, u * rows : (u + 1) * rows, :].astype(F32)
                x = xraw[s, c, me, :, q * blk : (q + 1) * blk].astype(F32)
                x = jnp.where(ok, x, zero)
                h = jnp.where(ok, level * x + y, zero)
                cols = slice(p * blk, (p + 1) * blk)
                hpsi_ref[s, :, cols] = h
                corr_ref[s, :, cols] = x
                xx = xx + x * x
                xh = xh + x * h
                bh = [bh[j] + basis_ref[j, s, :, cols] * h for j in range(nb)]
        return xx, xh, bh

    acc = (zero, zero, [zero] * nb)
    for s in range(sectors):
        for c in range(CHUNKS):
            assemble(s, c)
            first(s, c)
            if s + 1 < sectors:
                pass_on(s + 1, c)
        if s > 0:
            send_far(s - 1)
        second(s)
        mix()
        turn_out(s)
    basis_copy.wait()
    send_far(sectors - 1)
    for s in range(sectors):
        acc = finish(s, acc)
    xx, xh, bh = acc

    def whole(t):
        t = jnp.sum(jnp.sum(t, axis=0, keepdims=True), axis=1, keepdims=True)
        return jnp.broadcast_to(t, (1, blk))

    xx, xh, bh = whole(xx), whole(xh), [whole(b) for b in bh]
    q = xh / (xx + 1e-6)
    rr, xr = zero, zero
    for s in range(sectors):
        for p in range(size_p):
            cols = slice(p * blk, (p + 1) * blk)
            x = corr_ref[s, :, cols]
            r = hpsi_ref[s, :, cols] - q * x
            rr = rr + r * r
            xr = xr + x * r
    stats = jnp.concatenate(
        [xx, xh] + bh + [whole(rr), whole(xr), jnp.zeros((4 - nb, blk), F32)], axis=0
    )

    def spread(level_no, stats, slots, count, mine_at, target):
        tile[level_no] = stats
        slots[mine_at] = stats
        for j in range(1, count):
            pltpu.make_async_remote_copy(
                src_ref=tile.at[level_no],
                dst_ref=slots.at[mine_at],
                send_sem=send3.at[level_no],
                recv_sem=recv3.at[level_no],
                device_id=target(j),
                device_id_type=MESH,
            ).start()
        some = slots.at[pl.ds(0, count - 1)]
        pltpu.make_async_copy(some, some, recv3.at[level_no]).wait()
        pltpu.make_async_copy(some, some, send3.at[level_no]).wait()
        return merge(slots[...], nb)

    stats, q = spread(0, stats, slots_m, n, me, lambda j: (row, lax.rem(me + j, n)))
    stats, q = spread(1, stats, slots_s, groups, row, lambda j: (lax.rem(row + j, groups), me))
    stat_ref[...] = jnp.concatenate([q, stats[1:]], axis=0)
    scale = 1.0 / jnp.sqrt(stats[2 + nb : 3 + nb] / cells + 1e-6)
    for s in range(sectors):
        for p in range(size_p):
            cols = slice(p * blk, (p + 1) * blk)
            corr_ref[s, :, cols] = (hpsi_ref[s, :, cols] - q * corr_ref[s, :, cols]) * scale
    for copy in list(far.values()) + list(near.values()) + list(relay.values()):
        copy.wait_send()
    for copy in list(swaps.values()) + list(sends.values()):
        copy.wait_send()


def body(n, groups, psi, left_env, right_env, term_op, ops, energy, charge, block_dims, basis):
    sectors, rows, width = psi.shape
    _, terms, blk, _ = left_env.shape
    op_count, size_p, _ = ops.shape
    nb = basis.shape[0]
    chips = n // 2
    cells = float(sectors * groups * rows * n * width)
    pairs = -(-min(terms, (terms + op_count) // 2) // 4) * 4
    cw = width // CHUNKS
    pn = size_p // PARTS
    wide = size_p * SUB
    smem = pl.BlockSpec(memory_space=pltpu.SMEM)
    vmem = pl.BlockSpec(memory_space=pltpu.VMEM)
    far = pl.BlockSpec(memory_space=pl.ANY)
    dma = pltpu.SemaphoreType.DMA
    like = jax.ShapeDtypeStruct(psi.shape, F32)
    hops = max(chips - 1, 1)
    hpsi, correction, stats = pl.pallas_call(
        functools.partial(kernel, n, groups, cells, pairs),
        out_shape=(like, like, jax.ShapeDtypeStruct((8, blk), F32)),
        in_specs=[smem, smem, smem, smem, vmem, far, far, far, far],
        out_specs=(vmem, vmem, vmem),
        scratch_shapes=[
            pltpu.VMEM((sectors, CHUNKS, n, rows, cw), BF16),
            pltpu.VMEM((width, blk), BF16),
            pltpu.VMEM(left_env.shape, BF16),
            pltpu.VMEM(right_env.shape, BF16),
            pltpu.VMEM((sectors, blk, terms * blk), BF16),
            pltpu.VMEM((sectors, terms + 1, blk, blk), BF16),
            pltpu.VMEM((terms, blk, width), BF16),
            pltpu.VMEM((pairs + 1, size_p, blk, blk), F32),
            pltpu.VMEM((wide, 2 * op_count * wide), BF16),
            pltpu.VMEM((size_p, blk, blk), F32),
            pltpu.VMEM((sectors, size_p, blk, blk), F32),
            pltpu.VMEM((chips, sectors, PARTS, pn, rows, blk), F32),
            pltpu.VMEM((hops, sectors, PARTS, pn * rows, blk), BF16),
            pltpu.VMEM((hops, sectors, PARTS, pn * rows, blk), BF16),
            pltpu.VMEM(basis.shape, F32),
            pltpu.VMEM((8, 128), I32),
            pltpu.SMEM((8, 128), I32),
            pltpu.VMEM((n, 8, blk), F32),
            pltpu.VMEM((groups, 8, blk), F32),
            pltpu.VMEM((2, 8, blk), F32),
            dma((sectors, CHUNKS)),
            dma((2, sectors)),
            dma(()),
            dma(()),
            dma((chips, sectors * CHUNKS)),
            dma((chips, sectors * CHUNKS)),
            dma((chips, sectors * CHUNKS)),
            dma((chips, sectors * CHUNKS)),
            dma((chips, sectors * PARTS)),
            dma((chips, sectors * PARTS)),
            dma((chips, sectors * PARTS)),
            dma((chips, sectors * PARTS)),
            dma((2,)),
            dma((2,)),
        ],
        compiler_params=pltpu.CompilerParams(
            collective_id=0, has_side_effects=True, vmem_limit_bytes=61 * 2**20
        ),
        name="step",
    )(block_dims, charge, energy, term_op, ops, psi, left_env, right_env, basis)
    return (hpsi, correction, stats[0, 0], stats[2 : 2 + nb, 0])


def solution(mesh):
    placed = (
        P("sector", "mpo", None),
        P("sector", "mpo", None, None),
        P("sector", "mpo", None, None),
        P("mpo"),
        P(),
        P(),
        P("sector"),
        P("sector", None),
        P(None, "sector", "mpo", None),
    )
    return jax.shard_map(
        functools.partial(body, mesh.shape["mpo"], mesh.shape["sector"]),
        mesh=mesh,
        in_specs=placed,
        out_specs=(P("sector", "mpo", None), P("sector", "mpo", None), P(), P()),
        check_vma=False,
    )
```

```python
import functools

import jax
import jax.numpy as jnp
from jax import lax
from jax.experimental import pallas as pl
from jax.experimental.pallas import tpu as pltpu
from jax.sharding import PartitionSpec as P

MESH = pl.DeviceIdType.MESH
F32, BF16, I32 = jnp.float32, jnp.bfloat16, jnp.int32
SUB = 8
CHUNKS = 2
PARTS = 4
FLAT = 64


def term_table(op_ref, terms, pairs):
    lane = lax.broadcasted_iota(I32, (terms, 128), 1)
    sub = lax.broadcasted_iota(I32, (terms, 128), 0)
    lane1 = lax.broadcasted_iota(I32, (1, 128), 1)
    col = jnp.zeros((terms, 128), I32)
    row = jnp.full((1, 128), -1, I32)
    for k in range(terms):
        o = op_ref[k]
        col = jnp.where(sub == k, o, col)
        row = jnp.where(lane1 == k, o, row)
    row = jnp.broadcast_to(row, (terms, 128))
    one, zero = jnp.ones((terms, 128), I32), jnp.zeros((terms, 128), I32)

    def along(mask, axis):
        return jnp.sum(jnp.where(mask, one, zero), axis=axis, keepdims=True)

    same = col == row
    rank_col = jnp.broadcast_to(along(same & (lane < sub), 1), (terms, 128))
    rank_row = jnp.broadcast_to(along(same & (sub < lane), 0), (terms, 128))
    heads = (row >= 0) & ((rank_row & 1) == 0)
    base = jnp.broadcast_to(along((row < col) & heads, 1), (terms, 128))
    place = 2 * base + rank_col
    hit = place == lane
    index = jnp.sum(jnp.where(hit, sub, zero), axis=0, keepdims=True)
    valid = along(hit, 0) > 0
    start = along(hit & (rank_col == 0), 0) > 0
    even = (rank_col & 1) == 0
    own = along(even & (col == lane), 0)
    upto = along(even & (col <= lane), 0)
    right = jnp.where(valid, index, terms)
    prev = jnp.where(valid & jnp.logical_not(start), (lane1 >> 1) - 1, pairs)
    last = jnp.where(own > 0, upto - 1, pairs)
    return jnp.concatenate([index, right, prev, last, jnp.zeros((4, 128), I32)], axis=0)


def mixing(ops_ref, om_ref):
    op_count, size_p, _ = ops_ref.shape
    wide = size_p * SUB
    up = (
        lax.broadcasted_iota(I32, (wide, size_p), 0) // SUB
        == lax.broadcasted_iota(I32, (wide, size_p), 1)
    ).astype(F32).astype(BF16)
    across = (
        lax.broadcasted_iota(I32, (size_p, wide), 1) // SUB
        == lax.broadcasted_iota(I32, (size_p, wide), 0)
    ).astype(F32).astype(BF16)
    diagonal = (lax.broadcasted_iota(I32, (wide, wide), 0) % SUB) == (
        lax.broadcasted_iota(I32, (wide, wide), 1) % SUB
    )
    for o in range(op_count):
        t = jnp.dot(up, ops_ref[o], preferred_element_type=F32).astype(BF16)
        u = jnp.dot(t, across, preferred_element_type=F32)
        u = jnp.where(diagonal, u, jnp.zeros_like(u)).astype(BF16)
        om_ref[:, o * wide : (o + 1) * wide] = u
        om_ref[:, (op_count + o) * wide : (op_count + o + 1) * wide] = u


def merge(stats, nb):
    xx, xh = stats[:, 0:1], stats[:, 1:2]
    rr, xr = stats[:, 2 + nb : 3 + nb], stats[:, 3 + nb : 4 + nb]
    q = xh / (xx + 1e-6)
    total = jnp.sum(stats, axis=0)
    all_q = total[1:2] / (total[0:1] + 1e-6)
    gap = q - all_q[None]
    rr = jnp.sum(rr + 2.0 * gap * xr + gap * gap * xx, axis=0)
    xr = jnp.sum(xr + gap * xx, axis=0)
    return jnp.concatenate(
        [total[: 2 + nb], rr, xr, jnp.zeros((4 - nb, total.shape[1]), F32)], axis=0
    ), all_q


def kernel(
    n,
    groups,
    cells,
    pairs,
    dims_ref,
    charge_ref,
    energy_ref,
    op_ref,
    ops_ref,
    psi_hbm,
    left_hbm,
    right_hbm,
    basis_hbm,
    hpsi_ref,
    x_ref,
    stat_ref,
    xraw,
    xt,
    lt,
    rt,
    v_ref,
    sums,
    om_ref,
    part_ref,
    theirs,
    away,
    landed,
    basis_ref,
    tab_v,
    tab,
    slots_m,
    slots_s,
    tile,
    own_sem,
    env_sem,
    basis_sem,
    tab_sem,
    gsend,
    grecv,
    fsend,
    frecv,
    send1,
    recv1,
    send2,
    recv2,
    send3,
    recv3,
):
    row = lax.axis_index("sector")
    me = lax.axis_index("mpo")
    one_level = n * groups <= FLAT
    chips = n // 2
    core, chip = lax.rem(me, 2), lax.div(me, 2)
    sib = chip * 2 + 1 - core
    sectors, terms, blk, _ = left_hbm.shape
    rows, cw = xraw.shape[3:]
    size_p = part_ref.shape[1]
    op_count = ops_ref.shape[0]
    nb = basis_ref.shape[0]
    qn = cw // blk
    pn = size_p // PARTS
    width = size_p * blk

    def at(hop):
        return lax.rem(chip + hop, chips) * 2

    envs = {}
    for s in range(sectors):
        for i, src in enumerate((left_hbm, right_hbm)):
            envs[i, s] = pltpu.make_async_copy(
                src.at[s], v_ref.at[:, :, pl.ds((2 * s + i) * blk, blk)], env_sem.at[i, s]
            )
    own = {}
    for s in range(sectors):
        for c in range(CHUNKS):
            own[s, c] = pltpu.make_async_copy(
                psi_hbm.at[s, :, pl.ds(c * cw, cw)], xraw.at[s, c, me], own_sem.at[s, c]
            )
    barrier = pltpu.get_barrier_semaphore()
    for j in range(1, n):
        pl.semaphore_signal(
            barrier, inc=1, device_id=(row, lax.rem(me + j, n)), device_id_type=MESH
        )
    for i in range(1, groups):
        for j in range(n if one_level else 1):
            pl.semaphore_signal(
                barrier,
                inc=1,
                device_id=(lax.rem(row + i, groups), lax.rem(me + j, n)),
                device_id_type=MESH,
            )
    envs[0, 0].start()
    for copy in own.values():
        copy.start()
    envs[1, 0].start()
    for s in range(1, sectors):
        envs[0, s].start()
        envs[1, s].start()
    tab_v[...] = term_table(op_ref, terms, pairs)
    table = pltpu.make_async_copy(tab_v, tab, tab_sem)
    table.start()
    mixing(ops_ref, om_ref)
    pl.semaphore_wait(barrier, n * groups - 1 if one_level else n + groups - 2)

    def push(src, block, s, c, to, ssem, rsem):
        return pltpu.make_async_remote_copy(
            src_ref=src,
            dst_ref=xraw.at[s, c, block],
            send_sem=ssem,
            recv_sem=rsem,
            device_id=(row, to),
            device_id_type=MESH,
        )

    far, near, relay = {}, {}, {}
    for s in range(sectors):
        for c in range(CHUNKS):
            i = s * CHUNKS + c
            src = psi_hbm.at[s, :, pl.ds(c * cw, cw)]
            for hop in range(1, chips):
                far[hop, s, c] = push(
                    src, me, s, c, at(hop) + core, gsend.at[hop, i], grecv.at[hop, i]
                )
                far[hop, s, c].start()
            near[s, c] = push(src, me, s, c, sib, gsend.at[0, i], grecv.at[0, i])
            near[s, c].start()

    def pass_on(s, c):
        i = s * CHUNKS + c
        for hop in range(1, chips):
            far[hop, s, c].wait_recv()
            block = at(chips - hop) + core
            relay[hop, s, c] = push(
                xraw.at[s, c, block], block, s, c, sib, fsend.at[hop, i], frecv.at[hop, i]
            )
            relay[hop, s, c].start()

    def arrived(s, c):
        own[s, c].wait()
        near[s, c].wait_recv()
        for hop in range(1, chips):
            relay[hop, s, c].wait_recv()

    basis_copy = pltpu.make_async_copy(basis_hbm, basis_ref, basis_sem)
    basis_copy.start()
    sums[pairs] = jnp.zeros(sums.shape[1:], F32)

    def turn_left(s):
        envs[0, s].wait()

        def step(i, c):
            for u in range(4):
                k = i * 4 + u
                lt[s, :, pl.ds(pl.multiple_of(k * blk, blk), blk)] = v_ref[k, :, 2 * s * blk : (2 * s + 1) * blk].T
            return c

        lax.fori_loop(0, terms // 4, step, 0)

    def turn_right(s):
        envs[1, s].wait()

        def step(i, c):
            for u in range(4):
                k = i * 4 + u
                rt[s, k] = v_ref[k, :, (2 * s + 1) * blk : (2 * s + 2) * blk].T
            return c

        lax.fori_loop(0, terms // 4, step, 0)
        rt[s, terms] = jnp.zeros((blk, blk), BF16)

    turn_left(0)
    turn_right(0)
    for s in range(1, sectors):
        turn_left(s)
    pass_on(0, 0)
    for s in range(1, sectors):
        turn_right(s)
    table.wait()

    row_at = lax.broadcasted_iota(I32, (blk, blk), 0)
    col_at = lax.broadcasted_iota(I32, (blk, blk), 1)

    def assemble(s, c):
        arrived(s, c)
        ok = (row_at < dims_ref[s, 0]) & (col_at < dims_ref[s, 1])
        for q in range(qn):
            x = jnp.concatenate(
                [xraw[s, c, b, :, q * blk : (q + 1) * blk].astype(F32) for b in range(n)], axis=0
            )
            x = jnp.where(ok, x, jnp.zeros_like(x)).astype(BF16)
            xt[(c * qn + q) * blk : (c * qn + q + 1) * blk, :] = x.T

    def first(begin, count, s):
        some = next(k for k in (16, 8, 4, 2, 1) if terms % k == 0)

        def step(i, carry):
            m = jnp.dot(
                xt[begin : begin + count, :],
                lt[s, :, pl.ds(pl.multiple_of(i * some * blk, some * blk), some * blk)],
                preferred_element_type=F32,
            ).astype(BF16)
            for u in range(some):
                for q in range(count // blk):
                    v_ref[i * some + u, :, begin + q * blk : begin + (q + 1) * blk] = m[
                        q * blk : (q + 1) * blk, u * blk : (u + 1) * blk
                    ]
            return carry

        lax.fori_loop(0, terms // some, step, 0)

    def second(s):
        def step(i, carry):
            for u in range(4):
                j = i * 4 + u
                r = jnp.concatenate([rt[s, tab[1, 2 * j]], rt[s, tab[1, 2 * j + 1]]], axis=1)
                v = jnp.concatenate([v_ref[tab[0, 2 * j]], v_ref[tab[0, 2 * j + 1]]], axis=0)
                m = jnp.dot(r, v, preferred_element_type=F32)
                prev = tab[2, 2 * j]
                for q in range(size_p):
                    sums[j, q] = sums[prev, q] + m[:, q * blk : (q + 1) * blk]
            return carry

        lax.fori_loop(0, pairs // 4, step, 0)

    def mix(s):
        wide = size_p * SUB

        def step(i, carry):
            both = []
            for t in range(4):
                b0 = pl.multiple_of((i * 4 + t) * SUB, SUB)
                high, low = [], []
                for o in range(op_count):
                    y = sums[tab[3, o], :, pl.ds(b0, SUB), :].reshape(wide, blk)
                    h = y.astype(BF16)
                    high.append(h)
                    low.append((y - h.astype(F32)).astype(BF16))
                both.append(jnp.concatenate(high + low, axis=0))
            m = jnp.dot(om_ref[...], jnp.concatenate(both, axis=1), preferred_element_type=F32)
            for t in range(4):
                b0 = pl.multiple_of((i * 4 + t) * SUB, SUB)
                part_ref[s, :, pl.ds(b0, SUB), :] = m[:, t * blk : (t + 1) * blk].reshape(
                    size_p, SUB, blk
                )
            return carry

        lax.fori_loop(0, blk // (4 * SUB), step, 0)

    order = list(range(1, chips)) + [0]
    swaps, sends = {}, {}

    def rows_of(block):
        return pl.ds(pl.multiple_of(block * rows, rows), rows)

    def turn_out(s):
        for g in range(PARTS):
            for p in range(g * pn, (g + 1) * pn):
                part_ref[s, p] = part_ref[s, p].T
            for hop in order:
                swaps[hop, s, g] = pltpu.make_async_remote_copy(
                    src_ref=part_ref.at[s, pl.ds(g * pn, pn), rows_of(at(hop) + 1 - core)],
                    dst_ref=theirs.at[hop, s, g],
                    send_sem=send1.at[hop, s * PARTS + g],
                    recv_sem=recv1.at[hop, s * PARTS + g],
                    device_id=(row, sib),
                    device_id_type=MESH,
                )
                swaps[hop, s, g].start()

    def send_far(s):
        for g in range(PARTS):
            for hop in range(1, chips):
                swaps[hop, s, g].wait_recv()
                y = part_ref[s, g * pn : (g + 1) * pn, rows_of(at(hop) + core), :] + theirs[hop, s, g]
                away[hop - 1, s, g] = y.reshape(pn * rows, blk).astype(BF16)
                sends[hop, s, g] = pltpu.make_async_remote_copy(
                    src_ref=away.at[hop - 1, s, g],
                    dst_ref=landed.at[hop - 1, s, g],
                    send_sem=send2.at[hop, s * PARTS + g],
                    recv_sem=recv2.at[hop, s * PARTS + g],
                    device_id=(row, at(hop) + core),
                    device_id_type=MESH,
                )
                sends[hop, s, g].start()

    zero = jnp.zeros((rows, blk), F32)
    mine_row = me * rows + lax.broadcasted_iota(I32, (rows, blk), 0)
    mine_col = lax.broadcasted_iota(I32, (rows, blk), 1)

    def whole(t):
        t = jnp.sum(jnp.sum(t, axis=0, keepdims=True), axis=1, keepdims=True)
        return jnp.broadcast_to(t, (1, blk))

    def finish(s):
        xx, xh, bh = zero, zero, [zero] * nb
        ok = (mine_row < dims_ref[s, 0]) & (mine_col < dims_ref[s, 1])
        level = energy_ref[charge_ref[s]]
        for g in range(PARTS):
            swaps[0, s, g].wait_recv()
            for hop in range(1, chips):
                sends[hop, s, g].wait_recv()
            for u in range(pn):
                p = g * pn + u
                c, q = p // qn, p % qn
                y = part_ref[s, p, rows_of(me), :] + theirs[0, s, g, u]
                for hop in range(1, chips):
                    y = y + landed[hop - 1, s, g, u * rows : (u + 1) * rows, :].astype(F32)
                x = xraw[s, c, me, :, q * blk : (q + 1) * blk].astype(F32)
                x = jnp.where(ok, x, zero)
                h = jnp.where(ok, level * x + y, zero)
                cols = slice(p * blk, (p + 1) * blk)
                hpsi_ref[s, :, cols] = h
                x_ref[s, :, cols] = x
                xx = xx + x * x
                xh = xh + x * h
                bh = [bh[j] + basis_ref[j, s, :, cols] * h for j in range(nb)]
        xx, xh, bh = whole(xx), whole(xh), [whole(b) for b in bh]
        q = xh / (xx + 1e-6)
        rr, xr = zero, zero
        for p in range(size_p):
            cols = slice(p * blk, (p + 1) * blk)
            x = x_ref[s, :, cols]
            r = hpsi_ref[s, :, cols] - q * x
            rr = rr + r * r
            xr = xr + x * r
        return jnp.concatenate(
            [xx, xh] + bh + [whole(rr), whole(xr), jnp.zeros((4 - nb, blk), F32)], axis=0
        )

    for s in range(sectors):
        for c in range(CHUNKS):
            assemble(s, c)
            if s == 0:
                for later in range(1, CHUNKS) if c == 0 else ():
                    pass_on(0, later)
                first(c * cw, cw, s)
            if s + 1 < sectors:
                pass_on(s + 1, c)
        if s > 0:
            first(0, width, s)
        if s > 0:
            send_far(s - 1)
        second(s)
        mix(s)
        turn_out(s)
    basis_copy.wait()
    send_far(sectors - 1)
    stats, _ = merge(jnp.stack([finish(s) for s in range(sectors)]), nb)

    def spread(level_no, stats, slots, count, mine_at, target):
        tile[level_no] = stats
        slots[mine_at] = stats
        for j in range(1, count):
            pltpu.make_async_remote_copy(
                src_ref=tile.at[level_no],
                dst_ref=slots.at[mine_at],
                send_sem=send3.at[level_no],
                recv_sem=recv3.at[level_no],
                device_id=target(j),
                device_id_type=MESH,
            ).start()
        some = slots.at[pl.ds(0, count - 1)]
        pltpu.make_async_copy(some, some, recv3.at[level_no]).wait()
        pltpu.make_async_copy(some, some, send3.at[level_no]).wait()
        return merge(slots[...], nb)

    if one_level:
        mine = row * n + me

        def other(j):
            there = lax.rem(mine + j, n * groups)
            return lax.div(there, n), lax.rem(there, n)

        stats, q = spread(0, stats, slots_m, n * groups, mine, other)
    else:
        stats, q = spread(0, stats, slots_m, n, me, lambda j: (row, lax.rem(me + j, n)))
        stats, q = spread(
            1, stats, slots_s, groups, row, lambda j: (lax.rem(row + j, groups), me)
        )
    scale = 1.0 / jnp.sqrt(stats[2 + nb : 3 + nb] / cells + 1e-6)
    stat_ref[...] = jnp.concatenate([q, scale, stats[2:]], axis=0)
    for copy in list(far.values()) + list(near.values()) + list(relay.values()):
        copy.wait_send()
    for copy in list(swaps.values()) + list(sends.values()):
        copy.wait_send()


def out_kernel(h_ref, x_ref, stat_ref, hpsi_hbm, corr_hbm, ritz_ref, row_ref, corr, sem):
    sectors, rows, width = h_ref.shape
    blk = stat_ref.shape[1]
    nb = row_ref.shape[1]
    copies = [pltpu.make_async_copy(h_ref, hpsi_hbm, sem.at[sectors])]
    copies[0].start()
    q, scale = stat_ref[0:1, :], stat_ref[1:2, :]
    for s in range(sectors):
        for p in range(width // blk):
            cols = slice(p * blk, (p + 1) * blk)
            corr[s, :, cols] = (h_ref[s, :, cols] - q * x_ref[s, :, cols]) * scale
        copies.append(pltpu.make_async_copy(corr.at[s], corr_hbm.at[s], sem.at[s]))
        copies[-1].start()
    ritz_ref[...] = q[:, :1]
    lane = lax.broadcasted_iota(I32, (1, blk), 1)
    line = jnp.zeros((1, blk), F32)
    for j in range(nb):
        line = jnp.where(lane == j, stat_ref[2 + j : 3 + j, :], line)
    row_ref[...] = line[:, :nb]
    for copy in copies:
        copy.wait()


def write_out(hpsi, x, stats, nb):
    vmem = pl.BlockSpec(memory_space=pltpu.VMEM)
    far = pl.BlockSpec(memory_space=pl.ANY)
    like = jax.ShapeDtypeStruct(hpsi.shape, F32)
    hpsi, correction, ritz, line = pl.pallas_call(
        out_kernel,
        out_shape=(
            like,
            like,
            jax.ShapeDtypeStruct((1, 1), F32),
            jax.ShapeDtypeStruct((1, nb), F32),
        ),
        in_specs=[vmem, vmem, vmem],
        out_specs=(far, far, vmem, vmem),
        scratch_shapes=[
            pltpu.VMEM(hpsi.shape, F32),
            pltpu.SemaphoreType.DMA((hpsi.shape[0] + 1,)),
        ],
        compiler_params=pltpu.CompilerParams(vmem_limit_bytes=4 * 2**20),
        name="write_out",
    )(hpsi, x, stats)
    return (hpsi, correction, ritz.reshape(()), line.reshape(nb))


def body(n, groups, psi, left_env, right_env, term_op, ops, energy, charge, block_dims, basis):
    sectors, rows, width = psi.shape
    _, terms, blk, _ = left_env.shape
    op_count, size_p, _ = ops.shape
    nb = basis.shape[0]
    chips = n // 2
    cells = float(sectors * groups * rows * n * width)
    pairs = -(-min(terms, (terms + op_count) // 2) // 4) * 4
    cw = width // CHUNKS
    pn = size_p // PARTS
    wide = size_p * SUB
    smem = pl.BlockSpec(memory_space=pltpu.SMEM)
    vmem = pl.BlockSpec(memory_space=pltpu.VMEM)
    held = pl.BlockSpec(memory_space=pltpu.HBM)
    dma = pltpu.SemaphoreType.DMA
    like = pltpu.VMEM(psi.shape, F32)
    hops = max(chips - 1, 1)
    hpsi, x, stats = pl.pallas_call(
        functools.partial(kernel, n, groups, cells, pairs),
        out_shape=(like, like, pltpu.VMEM((8, blk), F32)),
        in_specs=[smem, smem, smem, smem, vmem, held, held, held, held],
        out_specs=(vmem, vmem, vmem),
        scratch_shapes=[
            pltpu.VMEM((sectors, CHUNKS, n, rows, cw), BF16),
            pltpu.VMEM((width, blk), BF16),
            pltpu.VMEM((sectors, blk, terms * blk), BF16),
            pltpu.VMEM((sectors, terms + 1, blk, blk), BF16),
            pltpu.VMEM((terms, blk, width), BF16),
            pltpu.VMEM((pairs + 1, size_p, blk, blk), F32),
            pltpu.VMEM((wide, 2 * op_count * wide), BF16),
            pltpu.VMEM((sectors, size_p, blk, blk), F32),
            pltpu.VMEM((chips, sectors, PARTS, pn, rows, blk), F32),
            pltpu.VMEM((hops, sectors, PARTS, pn * rows, blk), BF16),
            pltpu.VMEM((hops, sectors, PARTS, pn * rows, blk), BF16),
            pltpu.VMEM(basis.shape, F32),
            pltpu.VMEM((8, 128), I32),
            pltpu.SMEM((8, 128), I32),
            pltpu.VMEM((n * groups if n * groups <= FLAT else n, 8, blk), F32),
            pltpu.VMEM((groups, 8, blk), F32),
            pltpu.VMEM((2, 8, blk), F32),
            dma((sectors, CHUNKS)),
            dma((2, sectors)),
            dma(()),
            dma(()),
            dma((chips, sectors * CHUNKS)),
            dma((chips, sectors * CHUNKS)),
            dma((chips, sectors * CHUNKS)),
            dma((chips, sectors * CHUNKS)),
            dma((chips, sectors * PARTS)),
            dma((chips, sectors * PARTS)),
            dma((chips, sectors * PARTS)),
            dma((chips, sectors * PARTS)),
            dma((2,)),
            dma((2,)),
        ],
        compiler_params=pltpu.CompilerParams(
            collective_id=0, has_side_effects=True, vmem_limit_bytes=56 * 2**20
        ),
        name="step",
    )(block_dims, charge, energy, term_op, ops, psi, left_env, right_env, basis)
    return write_out(hpsi, x, stats, nb)


def solution(mesh):
    placed = (
        P("sector", "mpo", None),
        P("sector", "mpo", None, None),
        P("sector", "mpo", None, None),
        P("mpo"),
        P(),
        P(),
        P("sector"),
        P("sector", None),
        P(None, "sector", "mpo", None),
    )
    return jax.shard_map(
        functools.partial(body, mesh.shape["mpo"], mesh.shape["sector"]),
        mesh=mesh,
        in_specs=placed,
        out_specs=(P("sector", "mpo", None), P("sector", "mpo", None), P(), P()),
        check_vma=False,
    )
```
